256 devices in a mesh: pipe: 2 (over core), dp: 4 (over x), fsdp: 32 (over z, y).
Axes of the slice: x: 4, y: 4, z: 8, core: 2. Of those that a mesh axis runs over, the one named last changes fastest.
Arguments:
- incoming: bfloat16 [1024, 6144], P(('pipe', 'dp'), 'fsdp'), may hold values from -6 to 6
- cotangent: bfloat16 [1024, 6144], P(('pipe', 'dp'), 'fsdp'), may hold values from -6 to 6
- weights: bfloat16 [2, 3, 6144, 16384], P('pipe', None, 'dp', 'fsdp'), may hold values from -0.078125 to 0.078125
- token_rows: int32 [1024], P(('pipe', 'dp')), may hold values from 0 to 127, as said below
- row_count: int32 [8], P(('pipe', 'dp')), may hold values from 1 to 128, as said below
- gate: float32 [1024], P(('pipe', 'dp')), may hold values from 0.1 to 1
Outputs:
- d_input: bfloat16 [1024, 6144], P(('pipe', 'dp'), 'fsdp')
- weight_grad: bfloat16 [2, 3, 6144, 16384], P('pipe', None, 'dp', 'fsdp')
The draws below stay inside these ranges and needn't reach their ends.
Inputs may be any that keep to these rules, and one draw needn't show every extreme that they name: `token_rows`: in each group the 128 entries are a permutation of 0 to 127; the first row_count entries name the tokens routed to the expert. `row_count`: some group's count is 128 in every draw.
All inputs are finite; a program needn't handle non-finite values.
Results may differ from the reference program's by a relative error of at most 0.02.
Values may be sent and summed in bfloat16 or wider, within the bound.
A program may use at most 128 MiB of HBM per device.

```python
import math
import jax
import jax.numpy as jnp
from jax import lax

D = 6144
H = 16384
TOK_GRP = 128
LAYERS = 2
TOKENS = 1024
N_PIPE = 2
N_DP = 4
N_FSDP = 32


def draw_token_rows(key, part):
    groups = TOKENS // TOK_GRP
    scores = jax.random.randint(key, (groups, TOK_GRP), 0, 1 << 20, dtype=jnp.int32)
    scores = scores * TOK_GRP + jnp.arange(TOK_GRP, dtype=jnp.int32)[None, :]
    order = jnp.argsort(scores, axis=1, stable=True).astype(jnp.int32)
    return order.reshape(TOKENS)


def draw_row_count(key, part):
    groups = TOKENS // TOK_GRP
    first_key = jax.random.fold_in(key, 11)
    second_key = jax.random.fold_in(key, 23)
    counts = jax.random.randint(first_key, (groups,), 1, TOK_GRP + 1, dtype=jnp.int32)
    chosen = jax.random.randint(second_key, (), 0, groups, dtype=jnp.int32)
    positions = jnp.arange(groups, dtype=jnp.int32)
    return jnp.where(positions == chosen, TOK_GRP, counts).astype(jnp.int32)


def block_scale(own_key, dims, cuts, smallest, largest):
    def one(axis_at, parts):
        draws = jax.random.uniform(jax.random.fold_in(jax.random.fold_in(own_key, 6), axis_at), (parts,), jnp.float32, smallest / len(cuts), largest / len(cuts))
        return jnp.repeat(jnp.exp(draws), dims[axis_at] // parts).reshape((-1,) + (1,) * (len(dims) - axis_at - 1))

    level = one(*cuts[0])
    for cut in cuts[1:]:
        level = level * one(*cut)
    return level


def gaussian(stream_key, shape, width, most, split=(), kind=jnp.bfloat16):
    result = width * jax.random.normal(stream_key, shape, jnp.float32)
    if split:
        result = result * block_scale(stream_key, shape, split, -0.22, 0.18)
    return jnp.clip(result, -most, most).astype(kind)


def setup_inputs(seed: int = 0) -> dict:
    seeds = jax.random.split(jax.random.key(seed), 7)
    incoming = gaussian(seeds[0], (TOKENS, D), 1.0, 6.0, ((0, 8), (1, 32)))
    cotangent = gaussian(seeds[1], (TOKENS, D), 1.0, 6.0, ((0, 8), (1, 32)))
    weights = gaussian(seeds[2], (LAYERS, 3, D, H), D ** -0.5, 0.078125, ((0, 2), (2, 4), (3, 32)))
    token_rows = draw_token_rows(jax.random.fold_in(seeds[6], 71), 0)
    row_count = draw_row_count(jax.random.fold_in(seeds[6], 71), 0)
    gate = jnp.clip(jnp.exp(math.log(1.0) - 2.3025851 * jax.random.uniform(seeds[5], (TOKENS,), jnp.float32) ** block_scale(seeds[5], (TOKENS,), ((0, 8),), -0.2, 0.2)), 0.1, 1.0)
    return dict(incoming=incoming, cotangent=cotangent, weights=weights, token_rows=token_rows, row_count=row_count, gate=gate)


def group_terms(arrived, returned, panel, rows, limit, gate_row):
    hidden_local = H // N_FSDP
    routed = arrived[rows]
    gate_pre = jnp.dot(routed, panel[0], preferred_element_type=jnp.float32)
    up_pre = jnp.dot(routed, panel[1], preferred_element_type=jnp.float32)
    sigmoid_gate = jax.nn.sigmoid(gate_pre)
    activated = (gate_pre * sigmoid_gate * up_pre).astype(jnp.bfloat16)
    live = jnp.arange(TOK_GRP, dtype=jnp.int32)[:, None] < limit
    weighted = gate_row[rows][:, None] * returned[rows].astype(jnp.float32)
    scaled = jnp.where(live, weighted, 0.0).astype(jnp.bfloat16)
    d_act = jnp.dot(scaled, panel[2], preferred_element_type=jnp.float32)
    d_gate = (d_act * up_pre * sigmoid_gate * (1.0 + gate_pre * (1.0 - sigmoid_gate))).astype(jnp.bfloat16)
    d_up = (d_act * gate_pre * sigmoid_gate).astype(jnp.bfloat16)
    gate_parts = d_gate.reshape(TOK_GRP, N_FSDP, hidden_local).transpose(1, 0, 2)
    up_parts = d_up.reshape(TOK_GRP, N_FSDP, hidden_local).transpose(1, 0, 2)
    wgate_parts = panel[0].reshape(D, N_FSDP, hidden_local).transpose(1, 0, 2)
    wup_parts = panel[1].reshape(D, N_FSDP, hidden_local).transpose(1, 0, 2)

    def add_share(total, shares):
        part_gate, part_up, part_wgate, part_wup = shares
        share = jnp.dot(part_gate, part_wgate.T, preferred_element_type=jnp.float32)
        share = share + jnp.dot(part_up, part_wup.T, preferred_element_type=jnp.float32)
        rounded = lax.optimization_barrier(share.astype(jnp.bfloat16))
        return total + rounded.astype(jnp.float32), None

    summed, _ = lax.scan(add_share, jnp.zeros((TOK_GRP, D), jnp.float32), (gate_parts, up_parts, wgate_parts, wup_parts))
    d_input = jnp.zeros((TOK_GRP, D), jnp.bfloat16).at[rows].set(summed.astype(jnp.bfloat16))
    grad_gate = jnp.dot(routed.T, d_gate, preferred_element_type=jnp.float32)
    grad_up = jnp.dot(routed.T, d_up, preferred_element_type=jnp.float32)
    grad_down = jnp.dot(scaled.T, activated, preferred_element_type=jnp.float32)
    return d_input, jnp.stack([grad_gate, grad_up, grad_down])


def reference(incoming, cotangent, weights, token_rows, row_count, gate):
    arrived_all = jnp.roll(incoming.reshape(N_PIPE, N_DP, TOK_GRP, D), 1, axis=0)
    returned_all = cotangent.reshape(N_PIPE, N_DP, TOK_GRP, D)
    rows_all = token_rows.reshape(N_PIPE, N_DP, TOK_GRP).astype(jnp.int32)
    counts_all = row_count.reshape(N_PIPE, N_DP)
    gates_all = gate.reshape(N_PIPE, N_DP, TOK_GRP)
    inputs_out = []
    grads_out = []
    for section in range(N_PIPE):
        panel = weights[section]

        def group_step(total, members):
            arrived, returned, rows, limit, gate_row = members
            d_input, grad = group_terms(arrived, returned, panel, rows, limit, gate_row)
            return total + grad, d_input

        start_total = jnp.zeros((3, D, H), jnp.float32)
        total, d_inputs = lax.scan(group_step, start_total, (arrived_all[section], returned_all[section], rows_all[section], counts_all[section], gates_all[section]))
        inputs_out.append(d_inputs)
        grads_out.append(total.astype(jnp.bfloat16))
    d_input = jnp.stack(inputs_out).reshape(TOKENS, D)
    weight_grad = jnp.stack(grads_out)
    return d_input, weight_grad
```

```python
import functools

import jax
import jax.numpy as jnp
from jax import lax
from jax.experimental import pallas as pl
from jax.experimental.pallas import tpu as pltpu
from jax.sharding import PartitionSpec as P

NX, NY, NZ = 4, 4, 8
TOK = 128
COLS = 192
ROWS_D = 1536
HID = 512
CUT = 80
CHUNK = 48
F32 = jnp.float32
BF16 = jnp.bfloat16
MESH = pl.DeviceIdType.MESH
N_RECV = 160
N_SEND = 224


class Links:
    def __init__(self, send_sem, recv_sem, me):
        self.send_sem, self.recv_sem, self.me = send_sem, recv_sem, me
        self.recv_at, self.sent, self.n_sent = {}, [], 0

    def recv(self, key):
        at = self.recv_at.setdefault(key, len(self.recv_at))
        return self.recv_sem.at[at]

    def put(self, key, src, dst, to, is_self=None):
        send = self.send_sem.at[self.n_sent]
        self.n_sent += 1
        recv = self.recv(key)
        copy = pltpu.make_async_remote_copy(
            src_ref=src, dst_ref=dst, send_sem=send, recv_sem=recv,
            device_id=to, device_id_type=MESH)
        if is_self is None:
            copy.start()
        else:
            pl.when(jnp.logical_not(is_self))(copy.start)
            pl.when(is_self)(pltpu.make_async_copy(src, dst, recv).start)
        self.sent.append((copy, is_self))

    def take(self, key, dst):
        pltpu.make_async_remote_copy(
            src_ref=dst, dst_ref=dst, send_sem=self.send_sem.at[0], recv_sem=self.recv(key),
            device_id=self.me, device_id_type=MESH).wait_recv()

    def finish(self):
        for copy, is_self in self.sent:
            if is_self is None:
                copy.wait_send()
            else:
                pl.when(jnp.logical_not(is_self))(copy.wait_send)


def flip(block):
    return block.astype(F32).T


def kernel(inc_ref, cot_ref, w_hbm, rows_ref, count_ref, gate_ref, din_ref, wg_hbm,
           w, first, cols, flat, part, own, xin, d_all, share, yin, ysum, zin, zsum, fin, wg,
           send_sem, recv_sem, w_sem, wg_sem):
    p = lax.axis_index("pipe")
    x = lax.axis_index("dp")
    f = lax.axis_index("fsdp")
    z, y = lax.div(f, NY), lax.rem(f, NY)

    def dev(px, xx, yy, zz):
        return (px, xx, zz * NY + yy)

    def at_x(o):
        return lax.rem(x + o + NX, NX)

    def at_y(o):
        return lax.rem(y + o + NY, NY)

    def at_z(o):
        return lax.rem(z + o + NZ, NZ)

    def to_x(o):
        return dev(p, at_x(o), y, z)

    def to_y(o):
        return dev(p, x, at_y(o), z)

    def to_z(o):
        return dev(p, x, y, at_z(o))

    home_x, home_z = lax.div(z, 2), 2 * x + lax.rem(z, 2)
    relay = dev(1 - p, home_x, y, home_z)
    home = dev(p, home_x, y, home_z)
    home_self = jnp.logical_and(home_x == x, home_z == z)
    end_z = 2 * x + lax.div(z, NZ // 2)
    fin_self = end_z == z

    barrier = pltpu.get_barrier_semaphore()

    def greet(to):
        pl.semaphore_signal(barrier, inc=1, device_id=to, device_id_type=MESH)

    greet(relay)
    pl.when(jnp.logical_not(home_self))(lambda: greet(home))
    for o in range(1, NX):
        greet(to_x(o))
    for o in range(1, NY):
        greet(to_y(o))
    for o in range(1, NZ):
        greet(to_z(o))
    for j in range(4):
        to = dev(p, at_x(j), y, end_z)
        if j == 0:
            pl.when(jnp.logical_not(fin_self))(functools.partial(greet, to))
        else:
            greet(to)
        src_z = 4 * lax.rem(z, 2) + j
        same = jnp.logical_and(home_x == x, src_z == z)
        pl.when(jnp.logical_not(same))(functools.partial(greet, dev(p, home_x, y, src_z)))

    w_copies = [pltpu.make_async_copy(w_hbm.at[0, i], w.at[i], w_sem.at[i]) for i in range(3)]
    for copy in w_copies:
        copy.start()

    first[0, 0:128] = flip(inc_ref[:, 0:128]).astype(BF16)
    first[0, 128:192] = flip(inc_ref[:, 128:192]).astype(BF16)
    down = lax.broadcasted_iota(jnp.int32, (TOK, TOK), 0)
    across = lax.broadcasted_iota(jnp.int32, (TOK, TOK), 1)
    routed_here = jnp.logical_and(down == rows_ref[...], across < count_ref[...])
    live = jnp.sum(jnp.where(routed_here, 1.0, 0.0), axis=1, keepdims=True) > 0.5
    gate = jnp.sum(jnp.where(down == across, gate_ref[...], 0.0), axis=1, keepdims=True)
    scaled = jnp.where(live, gate * cot_ref[...].astype(F32), 0.0).astype(BF16)
    first[1, 0:128] = flip(scaled[:, 0:128]).astype(BF16)
    first[1, 128:192] = flip(scaled[:, 128:192]).astype(BF16)

    expected = 1 + (NX - 1) + (NY - 1) + (NZ - 1) + 8
    pl.semaphore_wait(barrier, expected + jnp.where(home_self, 0, 1) - jnp.where(fin_self, 2, 0))

    links = Links(send_sem, recv_sem, to_z(1))
    put, take = links.put, links.take

    put(("home", 0), first.at[0], cols.at[0, home_z, y], relay)
    put(("home", 1), first.at[1], cols.at[1, home_z, y], home, home_self)

    low = pl.ds(0, CUT)
    high = pl.ds(CUT, COLS - CUT)

    def gather_steps(a):
        buf = cols.at[a]

        def piece(j, o=0):
            return buf.at[at_z(j), at_y(o), high]

        def block(j, part_of=slice(None)):
            if part_of == slice(None):
                return buf.at[at_z(j), :, low]
            return buf.at[at_z(j), pl.ds(part_of.start, 2), low]

        def spread(j):
            put(("y", a, 3, j % NZ), piece(j), piece(j), to_y(1))
            put(("y", a, 1, j % NZ), piece(j), piece(j), to_y(-1))

        def hop(s):
            if s <= 4:
                put(("f", a, s), piece(1 - s), piece(1 - s), to_z(1))
            if s <= 3:
                put(("b", a, s), piece(s - 1), piece(s - 1), to_z(-1))

        def block_hop(s):
            if s <= 3:
                put(("bf", a, s), block(1 - s), block(1 - s), to_z(1))
                put(("bb", a, s), block(s - 1), block(s - 1), to_z(-1))
            else:
                put(("bf", a, s), block(1 - s, slice(0, 2)), block(1 - s, slice(0, 2)), to_z(1))
                put(("bb", a, s), block(s - 1, slice(2, 4)), block(s - 1, slice(2, 4)), to_z(-1))

        def forward_up(j):
            take(("y", a, 3, j % NZ), piece(j, -1))
            put(("y", a, 2, j % NZ), piece(j, -1), piece(j, -1), to_y(1))

        def forward_down(j):
            take(("y", a, 1, j % NZ), piece(j, 1))
            put(("y", a, 2, j % NZ), piece(j, 1), piece(j, 1), to_y(-1))

        def start():
            take(("home", a), buf.at[z, y])
            for o in (1, 3, 2):
                own_low = buf.at[z, y, low]
                put(("ly", a, (NY - o) % NY), own_low, own_low, to_y(o))
            hop(1)
            spread(0)

        def middle(s):
            take(("f", a, s), piece(-s))
            if s < 4:
                put(("f", a, s + 1), piece(-s), piece(-s), to_z(1))
            if s <= 3:
                take(("b", a, s), piece(s))
                if s < 3:
                    put(("b", a, s + 1), piece(s), piece(s), to_z(-1))
            if s == 1:
                for o in range(1, NY):
                    take(("ly", a, o), buf.at[z, at_y(o), low])
                block_hop(1)
            else:
                take(("bf", a, s - 1), block(1 - s))
                take(("bb", a, s - 1), block(s - 1))
                block_hop(s)
            spread(-s)
            if s <= 3:
                spread(s)
            if s >= 2:
                forward_up(1 - s)
            forward_down(s - 1)

        def close():
            forward_up(-4)
            take(("bf", a, 4), block(-4, slice(0, 2)))
            take(("bb", a, 4), block(4, slice(2, 4)))

        def drain():
            for j in range(-4, 4):
                if j >= 0:
                    take(("y", a, 3, j % NZ), piece(j, -1))
                else:
                    take(("y", a, 1, j % NZ), piece(j, 1))
                take(("y", a, 2, j % NZ), piece(j, 2))

        return [start] + [functools.partial(middle, s) for s in range(1, 5)] + [close, drain]

    def flatten(a):
        def one(g, _):
            turned = flip(cols[a, pl.ds(2 * g, 2)].reshape(ROWS_D, TOK)).astype(BF16)
            flat[pl.ds(pl.multiple_of(g * TOK, TOK), TOK), :] = turned
            return 0
        lax.fori_loop(0, NX, one, 0)

    def project(i):
        for t in range(2):
            span = slice(t * 256, t * 256 + 256)
            out = jnp.dot(flat[...], w[i, :, span], preferred_element_type=F32)
            part[:, i, :, span] = out.astype(BF16).reshape(NX, TOK, 256)

    def send_part(name, lo, n):
        for o in (2, 1, 3):
            put((name, NX - o), part.at[at_x(o), pl.ds(lo, n)], xin.at[NX - o - 1, pl.ds(lo, n)], to_x(o))

    def take_part(name, lo, n):
        for o in range(1, NX):
            take((name, o), xin.at[o - 1, pl.ds(lo, n)])

    def total(i):
        out = part[x, i].astype(F32)
        for o in range(1, NX):
            out = out + xin[o - 1, i].astype(F32)
        return out

    routed_steps, scaled_steps = gather_steps(0), gather_steps(1)
    routed_steps[0]()
    routed_steps[1]()
    for k in range(2, 7):
        scaled_steps[k - 2]()
        routed_steps[k]()
    for copy in w_copies:
        copy.wait()
    flatten(0)
    project(0)
    project(1)
    send_part("gu", 0, 2)
    scaled_steps[5]()
    scaled_steps[6]()
    flatten(1)
    project(2)
    send_part("d", 2, 1)

    take_part("gu", 0, 2)
    g_pre = total(0)
    u_pre = total(1)
    sigma = 1.0 / (1.0 + jnp.exp(-g_pre))
    silu = g_pre * sigma
    d_all[x, 2] = (silu * u_pre).astype(BF16)
    own[0] = u_pre * sigma * (1.0 + g_pre * (1.0 - sigma))
    own[1] = silu

    def send_rows(name, lo, n):
        for o in (2, 1, 3):
            mine = d_all.at[x, pl.ds(lo, n)]
            put((name, NX - o), mine, mine, to_x(o))

    take_part("d", 2, 1)
    d_act = total(2)
    d_all[x, 0] = (d_act * own[0]).astype(BF16)
    d_all[x, 1] = (d_act * own[1]).astype(BF16)
    send_rows("dgu", 0, 2)
    send_rows("act", 2, 1)

    nt = (((1,), (1,)), ((), ()))

    def make_share(n, g):
        for k in range(2):
            rows = slice(768 * k, 768 * k + 768)
            out = lax.dot_general(w[0, rows], d_all[g, 0], nt, preferred_element_type=F32)
            out = out + lax.dot_general(w[1, rows], d_all[g, 1], nt, preferred_element_type=F32)
            share[n, k] = out.astype(BF16).reshape(NY, COLS, TOK)
        for o in (2, 1, 3):
            put(("sy", n, NY - o), share.at[n, :, at_y(o)], yin.at[n, NY - o - 1], to_y(o))

    def reduce_y(n):
        out = share[n, :, y].astype(F32)
        for o in range(1, NY):
            take(("sy", n, o), yin.at[n, o - 1])
            out = out + yin[n, o - 1].astype(F32)
        ysum[n] = out.astype(BF16).reshape(NZ, CHUNK, TOK)
        for o in (4, 3, 5, 2, 6, 1, 7):
            put(("sz", n, NZ - o), ysum.at[n, at_z(o)], zin.at[n, NZ - o - 1], to_z(o))

    def reduce_z(n, o_x):
        out = ysum[n, z].astype(F32)
        for o in range(1, NZ):
            take(("sz", n, o), zin.at[n, o - 1])
            out = out + zin[n, o - 1].astype(F32)
        zsum[n] = out.astype(BF16)
        put(("end",), zsum.at[n], fin.at[lax.rem(z, 4)], dev(p, at_x(o_x), y, end_z),
            fin_self if o_x == 0 else None)

    def weight_grad(i):
        a = 0 if i < 2 else 1
        right = d_all[:, i].reshape(NX * TOK, HID)
        for k in range(2):
            for q in range(2):
                left = jnp.concatenate(
                    [cols[a, 2 * g + k, pl.ds(2 * q, 2)].reshape(384, TOK) for g in range(NX)], axis=1)
                out = jnp.dot(left, right, preferred_element_type=F32)
                wg[i, 768 * k + 384 * q:768 * k + 384 * q + 384] = out.astype(BF16)
        pltpu.make_async_copy(wg.at[i], wg_hbm.at[0, i], wg_sem.at[i]).start()

    order = (0, 1, 3, 2)
    for n, o in enumerate(order):
        if o:
            take(("dgu", o), d_all.at[at_x(o), pl.ds(0, 2)])
        make_share(n, at_x(o))
        if n >= 1:
            reduce_y(n - 1)
        if n >= 2:
            reduce_z(n - 2, order[n - 2])
    weight_grad(0)
    reduce_y(3)
    reduce_z(2, order[2])
    weight_grad(1)
    reduce_z(3, order[3])
    for o in range(1, NX):
        take(("act", o), d_all.at[at_x(o), pl.ds(2, 1)])
    weight_grad(2)
    take(("end",), fin)
    done = fin[...].reshape(COLS, TOK)
    din_ref[:, 0:128] = flip(done[0:128]).astype(BF16)
    din_ref[:, 128:192] = flip(done[128:192]).astype(BF16)
    links.finish()
    for i in range(3):
        pltpu.make_async_copy(wg.at[i], wg_hbm.at[0, i], wg_sem.at[i]).wait()
    assert len(links.recv_at) <= N_RECV and links.n_sent <= N_SEND


def on_device(incoming, cotangent, weights, token_rows, row_count, gate):
    vmem = pl.BlockSpec(memory_space=pltpu.VMEM)
    anywhere = pl.BlockSpec(memory_space=pl.ANY)
    return pl.pallas_call(
        kernel,
        out_shape=(jax.ShapeDtypeStruct((TOK, COLS), BF16),
                   jax.ShapeDtypeStruct((1, 3, ROWS_D, HID), BF16)),
        in_specs=[vmem, vmem, anywhere, vmem, vmem, vmem],
        out_specs=(vmem, anywhere),
        scratch_shapes=[
            pltpu.VMEM((3, ROWS_D, HID), BF16),
            pltpu.VMEM((2, COLS, TOK), BF16),
            pltpu.VMEM((2, NZ, NY, COLS, TOK), BF16),
            pltpu.VMEM((NX * TOK, ROWS_D), BF16),
            pltpu.VMEM((NX, 3, TOK, HID), BF16),
            pltpu.VMEM((2, TOK, HID), F32),
            pltpu.VMEM((NX - 1, 3, TOK, HID), BF16),
            pltpu.VMEM((NX, 3, TOK, HID), BF16),
            pltpu.VMEM((NX, 2, NY, COLS, TOK), BF16),
            pltpu.VMEM((NX, NY - 1, 2, COLS, TOK), BF16),
            pltpu.VMEM((NX, NZ, CHUNK, TOK), BF16),
            pltpu.VMEM((NX, NZ - 1, CHUNK, TOK), BF16),
            pltpu.VMEM((NX, CHUNK, TOK), BF16),
            pltpu.VMEM((NX, CHUNK, TOK), BF16),
            pltpu.VMEM((3, ROWS_D, HID), BF16),
            pltpu.SemaphoreType.DMA((N_SEND,)),
            pltpu.SemaphoreType.DMA((N_RECV,)),
            pltpu.SemaphoreType.DMA((3,)),
            pltpu.SemaphoreType.DMA((3,)),
        ],
        compiler_params=pltpu.CompilerParams(
            collective_id=0, has_side_effects=True, vmem_limit_bytes=50 << 20),
        cost_estimate=pl.CostEstimate(flops=6_400_000_000, bytes_accessed=10_000_000, transcendentals=65536),
        name="expert",
    )(incoming, cotangent, weights, token_rows.reshape(1, TOK), row_count.reshape(1, 1), gate.reshape(1, TOK))


def solution(mesh):
    return jax.shard_map(
        on_device,
        mesh=mesh,
        in_specs=(
            P(("pipe", "dp"), "fsdp"),
            P(("pipe", "dp"), "fsdp"),
            P("pipe", None, "dp", "fsdp"),
            P(("pipe", "dp")),
            P(("pipe", "dp")),
            P(("pipe", "dp")),
        ),
        out_specs=(P(("pipe", "dp"), "fsdp"), P("pipe", None, "dp", "fsdp")),
        check_vma=False,
    )
```

```python
import functools

import jax
import jax.numpy as jnp
from jax import lax
from jax.experimental import pallas as pl
from jax.experimental.pallas import tpu as pltpu
from jax.sharding import PartitionSpec as P

NX, NY, NZ = 4, 4, 8
TOK = 128
COLS = 192
ROWS_D = 1536
HID = 512
CUT = 80
CHUNK = 48
F32 = jnp.float32
BF16 = jnp.bfloat16
MESH = pl.DeviceIdType.MESH
N_RECV = 256
N_SEND = 288


class Links:
    def __init__(self, send_sem, recv_sem, me):
        self.send_sem, self.recv_sem, self.me = send_sem, recv_sem, me
        self.recv_at, self.sent, self.n_sent = {}, [], 0

    def recv(self, key):
        at = self.recv_at.setdefault(key, len(self.recv_at))
        return self.recv_sem.at[at]

    def put(self, key, src, dst, to, is_self=None):
        send = self.send_sem.at[self.n_sent]
        self.n_sent += 1
        recv = self.recv(key)
        copy = pltpu.make_async_remote_copy(
            src_ref=src, dst_ref=dst, send_sem=send, recv_sem=recv,
            device_id=to, device_id_type=MESH)
        if is_self is None:
            copy.start()
        else:
            pl.when(jnp.logical_not(is_self))(copy.start)
            pl.when(is_self)(pltpu.make_async_copy(src, dst, recv).start)
        self.sent.append((copy, is_self))

    def take(self, key, dst):
        pltpu.make_async_remote_copy(
            src_ref=dst, dst_ref=dst, send_sem=self.send_sem.at[0], recv_sem=self.recv(key),
            device_id=self.me, device_id_type=MESH).wait_recv()

    def finish(self):
        for copy, is_self in self.sent:
            if is_self is None:
                copy.wait_send()
            else:
                pl.when(jnp.logical_not(is_self))(copy.wait_send)


def flip(block):
    return block.astype(F32).T


def kernel(inc_hbm, cot_hbm, w_hbm, rows_hbm, count_ref, gate_hbm, din_ref, wg,
           w, first, rows_ref, gate_ref, cols, flat, part, own, via, xin, d_all, share, yin, ysum, zin, zsum, fin,
           send_sem, recv_sem, w_sem):
    p = lax.axis_index("pipe")
    x = lax.axis_index("dp")
    f = lax.axis_index("fsdp")
    z, y = lax.div(f, NY), lax.rem(f, NY)

    def dev(px, xx, yy, zz):
        return (px, xx, zz * NY + yy)

    def at_x(o):
        return lax.rem(x + o + NX, NX)

    def at_y(o):
        return lax.rem(y + o + NY, NY)

    def at_z(o):
        return lax.rem(z + o + NZ, NZ)

    def to_x(o):
        return dev(p, at_x(o), y, z)

    def to_y(o):
        return dev(p, x, at_y(o), z)

    def to_z(o):
        return dev(p, x, y, at_z(o))

    home_x, home_z = lax.div(z, 2), 2 * x + lax.rem(z, 2)
    relay = dev(1 - p, home_x, y, home_z)
    home = dev(p, home_x, y, home_z)
    home_self = jnp.logical_and(home_x == x, home_z == z)
    end_z = 2 * x + lax.div(z, NZ // 2)
    fin_self = end_z == z

    barrier = pltpu.get_barrier_semaphore()

    def greet(to):
        pl.semaphore_signal(barrier, inc=1, device_id=to, device_id_type=MESH)

    greet(relay)
    pl.when(jnp.logical_not(home_self))(lambda: greet(home))
    for o in range(1, NX):
        greet(to_x(o))
    for o in range(1, NY):
        greet(to_y(o))
    for o in range(1, NZ):
        greet(to_z(o))
    for j in range(4):
        to = dev(p, at_x(j), y, end_z)
        if j == 0:
            pl.when(jnp.logical_not(fin_self))(functools.partial(greet, to))
        else:
            greet(to)
        src_z = 4 * lax.rem(z, 2) + j
        same = jnp.logical_and(home_x == x, src_z == z)
        pl.when(jnp.logical_not(same))(functools.partial(greet, dev(p, home_x, y, src_z)))

    small = [pltpu.make_async_copy(cot_hbm, first.at[0], w_sem.at[3]),
             pltpu.make_async_copy(rows_hbm, rows_ref, w_sem.at[4]),
             pltpu.make_async_copy(gate_hbm, gate_ref, w_sem.at[5])]
    w_copies = [pltpu.make_async_copy(w_hbm.at[0, i], w.at[i], w_sem.at[i]) for i in range(3)]
    for copy in small + w_copies:
        copy.start()
    for copy in small:
        copy.wait()

    down = lax.broadcasted_iota(jnp.int32, (TOK, TOK), 0)
    across = lax.broadcasted_iota(jnp.int32, (TOK, TOK), 1)
    named = jnp.sum(jnp.where(down == across, rows_ref[...], 0).astype(F32), axis=1, keepdims=True)
    routed_here = jnp.logical_and(named == across.astype(F32), down < count_ref[...])
    live = jnp.sum(jnp.where(routed_here, 1.0, 0.0), axis=0, keepdims=True) > 0.5
    first[1] = jnp.where(live, gate_ref[...] * first[0].astype(F32), 0.0).astype(BF16)

    expected = 1 + (NX - 1) + (NY - 1) + (NZ - 1) + 8
    pl.semaphore_wait(barrier, expected + jnp.where(home_self, 0, 1) - jnp.where(fin_self, 2, 0))

    links = Links(send_sem, recv_sem, to_z(1))
    put, take = links.put, links.take

    put(("home", 0), inc_hbm, cols.at[0, home_z, y], relay)

    low = pl.ds(0, CUT)
    high = pl.ds(CUT, COLS - CUT)

    def gather_steps(a):
        buf = cols.at[a]

        def piece(j, o=0):
            return buf.at[at_z(j), at_y(o), high]

        def block(j, o):
            return buf.at[at_z(j), at_y(o), low]

        def spread(j):
            put(("y", a, 3, j % NZ), piece(j), piece(j), to_y(1))
            put(("y", a, 1, j % NZ), piece(j), piece(j), to_y(-1))

        def block_hop(s, o):
            if s <= 3 or o < 2:
                put(("bf", a, s, o), block(1 - s, o), block(1 - s, o), to_z(1))
            if s <= 3 or o >= 2:
                put(("bb", a, s, o), block(s - 1, o), block(s - 1, o), to_z(-1))

        def forward_up(j):
            take(("y", a, 3, j % NZ), piece(j, -1))
            put(("y", a, 2, j % NZ), piece(j, -1), piece(j, -1), to_y(1))

        def forward_down(j):
            take(("y", a, 1, j % NZ), piece(j, 1))
            put(("y", a, 2, j % NZ), piece(j, 1), piece(j, 1), to_y(-1))

        def start():
            take(("home", a), buf.at[z, y])
            for o in (1, 3, 2):
                put(("ly", a, NY - o), block(0, 0), block(0, 0), to_y(o))
            put(("f", a, 1), piece(0), piece(0), to_z(1))
            put(("b", a, 1), piece(0), piece(0), to_z(-1))
            block_hop(1, 0)
            spread(0)

        def middle(s):
            take(("f", a, s), piece(-s))
            if s < 4:
                put(("f", a, s + 1), piece(-s), piece(-s), to_z(1))
            if s <= 3:
                take(("b", a, s), piece(s))
                if s < 3:
                    put(("b", a, s + 1), piece(s), piece(s), to_z(-1))
            for o in (0, 1, 3, 2):
                if s == 1:
                    if o:
                        take(("ly", a, o), block(0, o))
                        block_hop(1, o)
                else:
                    take(("bf", a, s - 1, o), block(1 - s, o))
                    take(("bb", a, s - 1, o), block(s - 1, o))
                    block_hop(s, o)
            spread(-s)
            if s <= 3:
                spread(s)
            if s >= 2:
                forward_up(1 - s)
            forward_down(s - 1)

        def close():
            forward_up(-4)
            for o in range(NY):
                take(("bf" if o < 2 else "bb", a, 4, o), block(4, o))

        def drain():
            for j in (0, -1, 1, -2, 2, -3, 3, -4):
                if j >= 0:
                    take(("y", a, 3, j % NZ), piece(j, -1))
                else:
                    take(("y", a, 1, j % NZ), piece(j, 1))
                take(("y", a, 2, j % NZ), piece(j, 2))
                flatten(a, at_z(j))

        return [start] + [functools.partial(middle, s) for s in range(1, 5)] + [close, drain]

    def flatten(a, slot):
        turned = flip(cols[a, slot].reshape(NY * COLS, TOK)).astype(BF16)
        flat[lax.rem(slot, 2), pl.ds(pl.multiple_of(lax.div(slot, 2) * TOK, TOK), TOK), :] = turned

    def project(i):
        for t in range(2):
            span = slice(t * 256, t * 256 + 256)
            out = jnp.dot(flat[0], w[i, 0:768, span], preferred_element_type=F32)
            out = out + jnp.dot(flat[1], w[i, 768:1536, span], preferred_element_type=F32)
            part[:, i, :, span] = out.astype(BF16).reshape(NX, TOK, 256)

    upper, lower = pl.ds(0, TOK // 2), pl.ds(TOK // 2, TOK // 2)

    def part_out(i):
        put(("via", i, 3), part.at[at_x(2), i, upper], via.at[0, i], to_x(1))
        put(("via", i, 1), part.at[at_x(2), i, lower], via.at[1, i], to_x(-1))
        put(("part", i, 3, 1), part.at[at_x(1), i, lower], xin.at[0, i, lower], to_x(1))
        put(("part", i, 1, 0), part.at[at_x(-1), i, upper], xin.at[1, i, upper], to_x(-1))

    def part_on(i):
        take(("via", i, 3), via.at[0, i])
        right = part[at_x(1), i, 0:64].astype(F32) + via[0, i].astype(F32)
        part[at_x(1), i, 0:64] = right.astype(BF16)
        put(("part", i, 3, 0), part.at[at_x(1), i, upper], xin.at[0, i, upper], to_x(1))
        take(("via", i, 1), via.at[1, i])
        left = part[at_x(-1), i, 64:128].astype(F32) + via[1, i].astype(F32)
        part[at_x(-1), i, 64:128] = left.astype(BF16)
        put(("part", i, 1, 1), part.at[at_x(-1), i, lower], xin.at[1, i, lower], to_x(-1))

    def total(i):
        take(("part", i, 3, 1), xin.at[0, i, lower])
        take(("part", i, 1, 0), xin.at[1, i, upper])
        take(("part", i, 3, 0), xin.at[0, i, upper])
        take(("part", i, 1, 1), xin.at[1, i, lower])
        return part[x, i].astype(F32) + xin[0, i].astype(F32) + xin[1, i].astype(F32)

    def rows_out(i):
        mine = d_all.at[x, i]
        put(("row", i, 3), mine, mine, to_x(1))
        put(("row", i, 1), mine, mine, to_x(-1))

    def rows_on(i):
        take(("row", i, 3), d_all.at[at_x(-1), i])
        onward = d_all.at[at_x(-1), i, upper]
        put(("far", i, 0), onward, onward, to_x(1))
        take(("row", i, 1), d_all.at[at_x(1), i])
        onward = d_all.at[at_x(1), i, lower]
        put(("far", i, 1), onward, onward, to_x(-1))

    def rows_far(i):
        take(("far", i, 0), d_all.at[at_x(2), i, upper])
        take(("far", i, 1), d_all.at[at_x(2), i, lower])

    routed_steps, scaled_steps = gather_steps(0), gather_steps(1)
    routed_steps[0]()
    put(("home", 1), first.at[1], cols.at[1, home_z, y], home, home_self)
    routed_steps[1]()
    routed_steps[2]()
    for k in range(3, 6):
        scaled_steps[k - 3]()
        routed_steps[k]()
    for copy in w_copies:
        copy.wait()
    routed_steps[6]()
    project(0)
    part_out(0)
    scaled_steps[3]()
    project(1)
    part_out(1)
    scaled_steps[4]()
    part_on(0)
    scaled_steps[5]()
    part_on(1)
    scaled_steps[6]()
    project(2)
    part_out(2)

    g_pre = total(0)
    u_pre = total(1)
    sigma = 1.0 / (1.0 + jnp.exp(-g_pre))
    silu = g_pre * sigma
    d_all[x, 2] = (silu * u_pre).astype(BF16)
    own[0] = u_pre * sigma * (1.0 + g_pre * (1.0 - sigma))
    own[1] = silu
    part_on(2)
    d_act = total(2)
    d_all[x, 0] = (d_act * own[0]).astype(BF16)
    rows_out(0)
    d_all[x, 1] = (d_act * own[1]).astype(BF16)
    rows_out(1)
    rows_out(2)

    nt = (((1,), (1,)), ((), ()))

    def make_share(n, g):
        for k in range(2):
            rows = slice(768 * k, 768 * k + 768)
            out = lax.dot_general(w[0, rows], d_all[g, 0], nt, preferred_element_type=F32)
            out = out + lax.dot_general(w[1, rows], d_all[g, 1], nt, preferred_element_type=F32)
            share[n, k] = out.astype(BF16).reshape(NY, COLS, TOK)
        for o in (2, 1, 3):
            put(("sy", n, NY - o), share.at[n, :, at_y(o)], yin.at[n, NY - o - 1], to_y(o))

    def reduce_y(n):
        out = share[n, :, y].astype(F32)
        for o in range(1, NY):
            take(("sy", n, o), yin.at[n, o - 1])
            out = out + yin[n, o - 1].astype(F32)
        ysum[n] = out.astype(BF16).reshape(NZ, CHUNK, TOK)
        for o in (4, 3, 5, 2, 6, 1, 7):
            put(("sz", n, NZ - o), ysum.at[n, at_z(o)], zin.at[n, NZ - o - 1], to_z(o))

    def reduce_z(n, o_x):
        out = ysum[n, z].astype(F32)
        for o in range(1, NZ):
            take(("sz", n, o), zin.at[n, o - 1])
            out = out + zin[n, o - 1].astype(F32)
        zsum[n] = out.astype(BF16)
        put(("end",), zsum.at[n], fin.at[lax.rem(z, 4)], dev(p, at_x(o_x), y, end_z),
            fin_self if o_x == 0 else None)

    def weight_grad(i):
        a = 0 if i < 2 else 1
        right = d_all[:, i].reshape(NX * TOK, HID)
        for k in range(2):
            for q in range(2):
                left = jnp.concatenate(
                    [cols[a, 2 * g + k, pl.ds(2 * q, 2)].reshape(384, TOK) for g in range(NX)], axis=1)
                out = jnp.dot(left, right, preferred_element_type=F32)
                wg[0, i, 768 * k + 384 * q:768 * k + 384 * q + 384] = out.astype(BF16)

    order = (0, 1, 3, 2)
    make_share(0, x)
    rows_on(0)
    rows_on(1)
    make_share(1, at_x(1))
    reduce_y(0)
    make_share(2, at_x(-1))
    reduce_y(1)
    reduce_z(0, order[0])
    rows_on(2)
    rows_far(0)
    rows_far(1)
    make_share(3, at_x(2))
    reduce_y(2)
    reduce_z(1, order[1])
    weight_grad(0)
    reduce_y(3)
    reduce_z(2, order[2])
    weight_grad(1)
    reduce_z(3, order[3])
    rows_far(2)
    weight_grad(2)
    take(("end",), fin)
    din_ref[...] = fin[...].reshape(COLS, TOK)
    links.finish()
    assert len(links.recv_at) <= N_RECV and links.n_sent <= N_SEND


def in_hbm(array):
    return pltpu.with_memory_space_constraint(array, pltpu.HBM)


def on_device(incoming, cotangent, weights, token_rows, row_count, gate):
    vmem = pl.BlockSpec(memory_space=pltpu.VMEM)
    hbm = pl.BlockSpec(memory_space=pltpu.HBM)
    d_input, weight_grad = pl.pallas_call(
        kernel,
        out_shape=(jax.ShapeDtypeStruct((COLS, TOK), BF16),
                   jax.ShapeDtypeStruct((1, 3, ROWS_D, HID), BF16)),
        in_specs=[hbm, hbm, hbm, hbm, vmem, hbm],
        out_specs=(vmem, vmem),
        scratch_shapes=[
            pltpu.VMEM((3, ROWS_D, HID), BF16),
            pltpu.VMEM((2, COLS, TOK), BF16),
            pltpu.VMEM((1, TOK), jnp.int32),
            pltpu.VMEM((1, TOK), F32),
            pltpu.VMEM((2, NZ, NY, COLS, TOK), BF16),
            pltpu.VMEM((2, NX * TOK, ROWS_D // 2), BF16),
            pltpu.VMEM((NX, 3, TOK, HID), BF16),
            pltpu.VMEM((2, TOK, HID), F32),
            pltpu.VMEM((2, 3, TOK // 2, HID), BF16),
            pltpu.VMEM((2, 3, TOK, HID), BF16),
            pltpu.VMEM((NX, 3, TOK, HID), BF16),
            pltpu.VMEM((NX, 2, NY, COLS, TOK), BF16),
            pltpu.VMEM((NX, NY - 1, 2, COLS, TOK), BF16),
            pltpu.VMEM((NX, NZ, CHUNK, TOK), BF16),
            pltpu.VMEM((NX, NZ - 1, CHUNK, TOK), BF16),
            pltpu.VMEM((NX, CHUNK, TOK), BF16),
            pltpu.VMEM((NX, CHUNK, TOK), BF16),
            pltpu.SemaphoreType.DMA((N_SEND,)),
            pltpu.SemaphoreType.DMA((N_RECV,)),
            pltpu.SemaphoreType.DMA((6,)),
        ],
        compiler_params=pltpu.CompilerParams(
            collective_id=0, has_side_effects=True, vmem_limit_bytes=36 << 20),
        cost_estimate=pl.CostEstimate(flops=6_400_000_000, bytes_accessed=10_000_000, transcendentals=65536),
        name="expert",
    )(in_hbm(incoming.T), in_hbm(cotangent.T), in_hbm(weights), in_hbm(token_rows.reshape(1, TOK)),
      row_count.reshape(1, 1), in_hbm(gate.reshape(1, TOK)))
    return d_input.T, weight_grad


def solution(mesh):
    return jax.shard_map(
        on_device,
        mesh=mesh,
        in_specs=(
            P(("pipe", "dp"), "fsdp"),
            P(("pipe", "dp"), "fsdp"),
            P("pipe", None, "dp", "fsdp"),
            P(("pipe", "dp")),
            P(("pipe", "dp")),
            P(("pipe", "dp")),
        ),
        out_specs=(P(("pipe", "dp"), "fsdp"), P("pipe", None, "dp", "fsdp")),
        check_vma=False,
    )
```

```python
import functools

import jax
import jax.numpy as jnp
from jax import lax
from jax.experimental import pallas as pl
from jax.experimental.pallas import tpu as pltpu
from jax.sharding import PartitionSpec as P

NX, NY, NZ = 4, 4, 8
TOK = 128
COLS = 192
ROWS_D = 1536
HID = 512
CUT = 80
CHUNK = 48
F32 = jnp.float32
BF16 = jnp.bfloat16
MESH = pl.DeviceIdType.MESH
N_RECV = 256
N_SEND = 288


class Links:
    def __init__(self, send_sem, recv_sem, me):
        self.send_sem, self.recv_sem, self.me = send_sem, recv_sem, me
        self.recv_at, self.sent, self.n_sent = {}, [], 0

    def recv(self, key):
        at = self.recv_at.setdefault(key, len(self.recv_at))
        return self.recv_sem.at[at]

    def put(self, key, src, dst, to, is_self=None):
        send = self.send_sem.at[self.n_sent]
        self.n_sent += 1
        recv = self.recv(key)
        copy = pltpu.make_async_remote_copy(
            src_ref=src, dst_ref=dst, send_sem=send, recv_sem=recv,
            device_id=to, device_id_type=MESH)
        if is_self is None:
            copy.start()
        else:
            pl.when(jnp.logical_not(is_self))(copy.start)
            pl.when(is_self)(pltpu.make_async_copy(src, dst, recv).start)
        self.sent.append((copy, is_self))

    def take(self, key, dst):
        pltpu.make_async_remote_copy(
            src_ref=dst, dst_ref=dst, send_sem=self.send_sem.at[0], recv_sem=self.recv(key),
            device_id=self.me, device_id_type=MESH).wait_recv()

    def finish(self):
        for copy, is_self in self.sent:
            if is_self is None:
                copy.wait_send()
            else:
                pl.when(jnp.logical_not(is_self))(copy.wait_send)


def flip(block):
    return block.astype(F32).T


def kernel(inc_hbm, cot_hbm, w_hbm, rows_hbm, count_ref, gate_hbm, din_ref, wg,
           w, first, rows_ref, gate_ref, cols, flat, part, own, via, xin, d_all, share, yin, ysum, zin, zsum, fin,
           send_sem, recv_sem, w_sem):
    p = lax.axis_index("pipe")
    x = lax.axis_index("dp")
    f = lax.axis_index("fsdp")
    z, y = lax.div(f, NY), lax.rem(f, NY)

    def dev(px, xx, yy, zz):
        return (px, xx, zz * NY + yy)

    def at_x(o):
        return lax.rem(x + o + NX, NX)

    def at_y(o):
        return lax.rem(y + o + NY, NY)

    def at_z(o):
        return lax.rem(z + o + NZ, NZ)

    def to_x(o):
        return dev(p, at_x(o), y, z)

    def to_y(o):
        return dev(p, x, at_y(o), z)

    def to_z(o):
        return dev(p, x, y, at_z(o))

    def slot_of(plane, m, k):
        return lax.rem(2 * plane + NZ + (1 + m if k else -m), NZ)

    def slot_holds(plane, slot):
        back = lax.rem(2 * plane + NZ - slot, NZ)
        k = (back > 3).astype(jnp.int32)
        m = jnp.where(back > 3, NZ - 1 - back, back)
        return lax.rem(plane + m, NX), k

    home_x = lax.div(z, 2)
    away = lax.rem(x - home_x + NX, NX)
    home_z = jnp.where(lax.rem(z, 2) == 1, lax.rem(z + away, NZ), lax.rem(z - away + NZ, NZ))
    from_x, from_k = slot_holds(x, z)
    from_z = 2 * x + from_k
    home_self = home_x == x
    end_z = 2 * x + lax.div(z, NZ // 2)
    fin_self = end_z == z

    barrier = pltpu.get_barrier_semaphore()

    def greet(to):
        pl.semaphore_signal(barrier, inc=1, device_id=to, device_id_type=MESH)

    relay = dev(1 - p, home_x, y, home_z)
    home = dev(p, home_x, y, home_z)
    greet(relay)
    greet(dev(1 - p, from_x, y, from_z))

    @pl.when(jnp.logical_not(home_self))
    def _():
        greet(home)
        greet(dev(p, from_x, y, from_z))
    for o in range(1, NX):
        greet(to_x(o))
    for o in range(1, NY):
        greet(to_y(o))
    for o in range(1, NZ):
        greet(to_z(o))
    for j in range(4):
        to = dev(p, at_x(j), y, end_z)
        if j == 0:
            pl.when(jnp.logical_not(fin_self))(functools.partial(greet, to))
        else:
            greet(to)
        src_z = 4 * lax.rem(z, 2) + j
        same = jnp.logical_and(home_x == x, src_z == z)
        pl.when(jnp.logical_not(same))(functools.partial(greet, dev(p, home_x, y, src_z)))

    small = [pltpu.make_async_copy(cot_hbm, first.at[0], w_sem.at[3]),
             pltpu.make_async_copy(rows_hbm, rows_ref, w_sem.at[4]),
             pltpu.make_async_copy(gate_hbm, gate_ref, w_sem.at[5])]
    w_copies = [pltpu.make_async_copy(w_hbm.at[0, i], w.at[i], w_sem.at[i]) for i in range(3)]
    for copy in small + w_copies:
        copy.start()
    expected = 2 + (NX - 1) + (NY - 1) + (NZ - 1) + 8
    pl.semaphore_wait(barrier, expected + jnp.where(home_self, 0, 2) - jnp.where(fin_self, 2, 0))

    links = Links(send_sem, recv_sem, to_z(1))
    put, take = links.put, links.take

    put(("home", 0), inc_hbm, cols.at[0, home_z, y], relay)

    for copy in small:
        copy.wait()

    down = lax.broadcasted_iota(jnp.int32, (TOK, TOK), 0)
    across = lax.broadcasted_iota(jnp.int32, (TOK, TOK), 1)
    named = jnp.sum(jnp.where(down == across, rows_ref[...], 0).astype(F32), axis=1, keepdims=True)
    routed_here = jnp.logical_and(named == across.astype(F32), down < count_ref[...])
    live = jnp.sum(jnp.where(routed_here, 1.0, 0.0), axis=0, keepdims=True) > 0.5
    first[1] = jnp.where(live, gate_ref[...] * first[0].astype(F32), 0.0).astype(BF16)

    low = pl.ds(0, CUT)
    high = pl.ds(CUT, COLS - CUT)

    def gather_steps(a):
        buf = cols.at[a]
        mid = CUT + 16 * ((COLS - CUT + 16) // 32)
        halves = (pl.ds(CUT, mid - CUT), pl.ds(mid, COLS - mid))

        def piece(j, o=0, rows=high):
            return buf.at[at_z(j), at_y(o), rows]

        def send_z(name, j, d, o, rows):
            put((name, a, (j - d) % NZ, o, rows.start), piece(j, o, rows), piece(j, o, rows), to_z(d))

        def take_z(name, j, o, rows):
            take((name, a, j % NZ, o, rows.start), piece(j, o, rows))

        def spread(j):
            for o in (2, 1, 3):
                put(("y", a, NY - o, j % NZ), piece(j), piece(j), to_y(o))

        def hop_out(o, rows):
            for d in (2, -2, 1, -1):
                send_z("z", 0, d, o, rows)

        def hop_on(o, rows, j):
            take_z("z", j, o, rows)
            d = 1 if j < 0 else -1
            send_z("z", j, d, o, rows)
            if rows is low:
                if (j < 0) == (o < 2):
                    send_z("z", j, 2 * d, o, rows)
            else:
                send_z("z", j, 2 * d, o, halves[0] if j < 0 else halves[1])

        def start():
            take(("home", a), buf.at[z, y])
            hop_out(0, high)
            for o in (2, 1, 3):
                put(("ly", a, NY - o), piece(0, 0, low), piece(0, 0, low), to_y(o))
            hop_out(0, low)
            spread(0)

        def first_hop():
            hop_on(0, high, -2)
            hop_on(0, high, 2)
            for o in (1, 3, 2):
                take(("ly", a, o), piece(0, o, low))
                hop_out(o, low)
            spread(-2)
            spread(2)
            for j in (-1, 1):
                take_z("z", j, 0, high)
                spread(j)
            hop_on(0, low, -2)
            hop_on(0, low, 2)

        def second_hop():
            for j in (-3, 3):
                take_z("z", j, 0, high)
                spread(j)
            for rows in halves:
                take_z("z", 4, 0, rows)
            spread(4)
            for o in (1, 3, 2):
                hop_on(o, low, -2)
                hop_on(o, low, 2)

        def close():
            for o in (0, 1, 3, 2):
                for j in (-1, 1, -3, 3, 4):
                    take_z("z", j, o, low)
            for j in (0, -2, 2, -1, 1, -3, 3, 4):
                for o in (1, 3, 2):
                    take(("y", a, o, j % NZ), piece(j, o))
                flatten(a, at_z(j))

        return [start, first_hop, second_hop, close]

    def flatten(a, slot):
        turned = flip(cols[a, slot].reshape(NY * COLS, TOK)).astype(BF16)
        g, k = slot_holds(x, slot)
        flat[k, pl.ds(pl.multiple_of(g * TOK, TOK), TOK), :] = turned

    def project(i):
        for t in range(2):
            span = slice(t * 256, t * 256 + 256)
            out = jnp.dot(flat[0], w[i, 0:768, span], preferred_element_type=F32)
            out = out + jnp.dot(flat[1], w[i, 768:1536, span], preferred_element_type=F32)
            part[:, i, :, span] = out.astype(BF16).reshape(NX, TOK, 256)

    upper, lower = pl.ds(0, TOK // 2), pl.ds(TOK // 2, TOK // 2)

    def part_out(i):
        put(("via", i, 3), part.at[at_x(2), i, upper], via.at[0, i], to_x(1))
        put(("via", i, 1), part.at[at_x(2), i, lower], via.at[1, i], to_x(-1))
        put(("part", i, 3, 1), part.at[at_x(1), i, lower], xin.at[0, i, lower], to_x(1))
        put(("part", i, 1, 0), part.at[at_x(-1), i, upper], xin.at[1, i, upper], to_x(-1))

    def part_on(i):
        take(("via", i, 3), via.at[0, i])
        right = part[at_x(1), i, 0:64].astype(F32) + via[0, i].astype(F32)
        part[at_x(1), i, 0:64] = right.astype(BF16)
        put(("part", i, 3, 0), part.at[at_x(1), i, upper], xin.at[0, i, upper], to_x(1))
        take(("via", i, 1), via.at[1, i])
        left = part[at_x(-1), i, 64:128].astype(F32) + via[1, i].astype(F32)
        part[at_x(-1), i, 64:128] = left.astype(BF16)
        put(("part", i, 1, 1), part.at[at_x(-1), i, lower], xin.at[1, i, lower], to_x(-1))

    def total(i):
        take(("part", i, 3, 1), xin.at[0, i, lower])
        take(("part", i, 1, 0), xin.at[1, i, upper])
        take(("part", i, 3, 0), xin.at[0, i, upper])
        take(("part", i, 1, 1), xin.at[1, i, lower])
        return part[x, i].astype(F32) + xin[0, i].astype(F32) + xin[1, i].astype(F32)

    def rows_out(i):
        mine = d_all.at[x, i]
        put(("row", i, 3), mine, mine, to_x(1))
        put(("row", i, 1), mine, mine, to_x(-1))

    def rows_on(i):
        take(("row", i, 3), d_all.at[at_x(-1), i])
        onward = d_all.at[at_x(-1), i, upper]
        put(("far", i, 0), onward, onward, to_x(1))
        take(("row", i, 1), d_all.at[at_x(1), i])
        onward = d_all.at[at_x(1), i, lower]
        put(("far", i, 1), onward, onward, to_x(-1))

    def rows_far(i):
        take(("far", i, 0), d_all.at[at_x(2), i, upper])
        take(("far", i, 1), d_all.at[at_x(2), i, lower])

    routed_steps, scaled_steps = gather_steps(0), gather_steps(1)
    routed_steps[0]()
    put(("home", 1), first.at[1], cols.at[1, home_z, y], home, home_self)
    routed_steps[1]()
    scaled_steps[0]()
    routed_steps[2]()
    scaled_steps[1]()
    for copy in w_copies:
        copy.wait()
    routed_steps[3]()
    project(0)
    part_out(0)
    project(1)
    part_out(1)
    scaled_steps[2]()
    part_on(0)
    part_on(1)
    scaled_steps[3]()
    project(2)
    part_out(2)

    g_pre = total(0)
    u_pre = total(1)
    sigma = 1.0 / (1.0 + jnp.exp(-g_pre))
    silu = g_pre * sigma
    d_all[x, 2] = (silu * u_pre).astype(BF16)
    own[0] = u_pre * sigma * (1.0 + g_pre * (1.0 - sigma))
    own[1] = silu
    part_on(2)
    d_act = total(2)
    d_all[x, 0] = (d_act * own[0]).astype(BF16)
    rows_out(0)
    d_all[x, 1] = (d_act * own[1]).astype(BF16)
    rows_out(1)

    nt = (((1,), (1,)), ((), ()))

    def make_share(n, g):
        for k in range(2):
            rows = slice(768 * k, 768 * k + 768)
            out = lax.dot_general(w[0, rows], d_all[g, 0], nt, preferred_element_type=F32)
            out = out + lax.dot_general(w[1, rows], d_all[g, 1], nt, preferred_element_type=F32)
            share[n, k] = out.astype(BF16).reshape(NY, COLS, TOK)
        if n == 3:
            for o in (2, 1, 3):
                put(("sy", n, NY - o), share.at[n, :, at_y(o)], yin.at[n, NY - o - 1], to_y(o))
        else:
            put(("sv", n, 3), share.at[n, 0, at_y(2)], yin.at[n, 1, 0], to_y(1))
            put(("sv", n, 1), share.at[n, 1, at_y(2)], yin.at[n, 1, 1], to_y(-1))
            put(("sy", n, 3, 1), share.at[n, 1, at_y(1)], yin.at[n, 2, 1], to_y(1))
            put(("sy", n, 1, 0), share.at[n, 0, at_y(-1)], yin.at[n, 0, 0], to_y(-1))

    def share_on(n):
        for k, o in ((0, 1), (1, -1)):
            take(("sv", n, 2 + o if k == 0 else 1), yin.at[n, 1, k])
            out = share[n, k, at_y(o)].astype(F32) + yin[n, 1, k].astype(F32)
            share[n, k, at_y(o)] = out.astype(BF16)
            put(("sy", n, 3 if o == 1 else 1, k), share.at[n, k, at_y(o)], yin.at[n, 2 if o == 1 else 0, k], to_y(o))

    def reduce_y(n):
        out = share[n, :, y].astype(F32)
        if n == 3:
            for o in range(1, NY):
                take(("sy", n, o), yin.at[n, o - 1])
                out = out + yin[n, o - 1].astype(F32)
        else:
            for o in (1, 3):
                take(("sy", n, o, 0), yin.at[n, o - 1, 0])
                take(("sy", n, o, 1), yin.at[n, o - 1, 1])
                out = out + yin[n, o - 1].astype(F32)
        ysum[n] = out.astype(BF16).reshape(NZ, CHUNK, TOK)
        for o in (4, 3, 5, 2, 6, 1, 7):
            put(("sz", n, NZ - o), ysum.at[n, at_z(o)], zin.at[n, NZ - o - 1], to_z(o))

    def reduce_z(n, o_x):
        out = ysum[n, z].astype(F32)
        for o in range(1, NZ):
            take(("sz", n, o), zin.at[n, o - 1])
            out = out + zin[n, o - 1].astype(F32)
        zsum[n] = out.astype(BF16)
        put(("end",), zsum.at[n], fin.at[lax.rem(z, 4)], dev(p, at_x(o_x), y, end_z),
            fin_self if o_x == 0 else None)

    def weight_grad(i):
        a = 0 if i < 2 else 1
        right = jnp.concatenate([d_all[at_x(m), i] for m in range(NX)], axis=0)
        for k in range(2):
            for q in range(2):
                left = jnp.concatenate(
                    [cols[a, slot_of(x, m, k), pl.ds(2 * q, 2)].reshape(384, TOK) for m in range(NX)], axis=1)
                out = jnp.dot(left, right, preferred_element_type=F32)
                wg[0, i, 768 * k + 384 * q:768 * k + 384 * q + 384] = out.astype(BF16)

    order = (0, 1, 3, 2)
    make_share(0, x)
    rows_on(0)
    rows_on(1)
    rows_out(2)
    share_on(0)
    make_share(1, at_x(1))
    make_share(2, at_x(-1))
    reduce_y(0)
    share_on(1)
    share_on(2)
    rows_far(0)
    rows_far(1)
    make_share(3, at_x(2))
    rows_on(2)
    reduce_y(1)
    reduce_y(2)
    reduce_z(0, order[0])
    weight_grad(0)
    reduce_y(3)
    reduce_z(1, order[1])
    reduce_z(2, order[2])
    weight_grad(1)
    reduce_z(3, order[3])
    rows_far(2)
    weight_grad(2)
    take(("end",), fin)
    din_ref[...] = fin[...].reshape(COLS, TOK)
    links.finish()
    assert len(links.recv_at) <= N_RECV and links.n_sent <= N_SEND


def in_hbm(array):
    return pltpu.with_memory_space_constraint(array, pltpu.HBM)


def on_device(incoming, cotangent, weights, token_rows, row_count, gate):
    vmem = pl.BlockSpec(memory_space=pltpu.VMEM)
    hbm = pl.BlockSpec(memory_space=pltpu.HBM)
    d_input, weight_grad = pl.pallas_call(
        kernel,
        out_shape=(jax.ShapeDtypeStruct((COLS, TOK), BF16),
                   jax.ShapeDtypeStruct((1, 3, ROWS_D, HID), BF16)),
        in_specs=[hbm, hbm, hbm, hbm, vmem, hbm],
        out_specs=(vmem, vmem),
        scratch_shapes=[
            pltpu.VMEM((3, ROWS_D, HID), BF16),
            pltpu.VMEM((2, COLS, TOK), BF16),
            pltpu.VMEM((1, TOK), jnp.int32),
            pltpu.VMEM((1, TOK), F32),
            pltpu.VMEM((2, NZ, NY, COLS, TOK), BF16),
            pltpu.VMEM((2, NX * TOK, ROWS_D // 2), BF16),
            pltpu.VMEM((NX, 3, TOK, HID), BF16),
            pltpu.VMEM((2, TOK, HID), F32),
            pltpu.VMEM((2, 3, TOK // 2, HID), BF16),
            pltpu.VMEM((2, 3, TOK, HID), BF16),
            pltpu.VMEM((NX, 3, TOK, HID), BF16),
            pltpu.VMEM((NX, 2, NY, COLS, TOK), BF16),
            pltpu.VMEM((NX, NY - 1, 2, COLS, TOK), BF16),
            pltpu.VMEM((NX, NZ, CHUNK, TOK), BF16),
            pltpu.VMEM((NX, NZ - 1, CHUNK, TOK), BF16),
            pltpu.VMEM((NX, CHUNK, TOK), BF16),
            pltpu.VMEM((NX, CHUNK, TOK), BF16),
            pltpu.SemaphoreType.DMA((N_SEND,)),
            pltpu.SemaphoreType.DMA((N_RECV,)),
            pltpu.SemaphoreType.DMA((6,)),
        ],
        compiler_params=pltpu.CompilerParams(
            collective_id=0, has_side_effects=True, vmem_limit_bytes=36 << 20),
        cost_estimate=pl.CostEstimate(flops=6_400_000_000, bytes_accessed=10_000_000, transcendentals=65536),
        name="expert",
    )(in_hbm(incoming.T), in_hbm(cotangent.T), in_hbm(weights), in_hbm(token_rows.reshape(1, TOK)),
      row_count.reshape(1, 1), in_hbm(gate.reshape(1, TOK)))
    return d_input.T, weight_grad


def solution(mesh):
    return jax.shard_map(
        on_device,
        mesh=mesh,
        in_specs=(
            P(("pipe", "dp"), "fsdp"),
            P(("pipe", "dp"), "fsdp"),
            P("pipe", None, "dp", "fsdp"),
            P(("pipe", "dp")),
            P(("pipe", "dp")),
            P(("pipe", "dp")),
        ),
        out_specs=(P(("pipe", "dp"), "fsdp"), P("pipe", None, "dp", "fsdp")),
        check_vma=False,
    )
```

```python
import functools

import jax
import jax.numpy as jnp
from jax import lax
from jax.experimental import pallas as pl
from jax.experimental.pallas import tpu as pltpu
from jax.sharding import PartitionSpec as P

NX, NY, NZ = 4, 4, 8
TOK = 128
COLS = 192
ROWS_D = 1536
HID = 512
CUT = 64
CHUNK = 48
F32 = jnp.float32
BF16 = jnp.bfloat16
MESH = pl.DeviceIdType.MESH
N_RECV = 256
N_SEND = 288


class Links:
    def __init__(self, send_sem, recv_sem, me):
        self.send_sem, self.recv_sem, self.me = send_sem, recv_sem, me
        self.recv_at, self.sent, self.n_sent = {}, [], 0

    def recv(self, key):
        at = self.recv_at.setdefault(key, len(self.recv_at))
        return self.recv_sem.at[at]

    def put(self, key, src, dst, to, is_self=None):
        send = self.send_sem.at[self.n_sent]
        self.n_sent += 1
        recv = self.recv(key)
        copy = pltpu.make_async_remote_copy(
            src_ref=src, dst_ref=dst, send_sem=send, recv_sem=recv,
            device_id=to, device_id_type=MESH)
        if is_self is None:
            copy.start()
        else:
            pl.when(jnp.logical_not(is_self))(copy.start)
            pl.when(is_self)(pltpu.make_async_copy(src, dst, recv).start)
        self.sent.append((copy, is_self))

    def take(self, key, dst):
        pltpu.make_async_remote_copy(
            src_ref=dst, dst_ref=dst, send_sem=self.send_sem.at[0], recv_sem=self.recv(key),
            device_id=self.me, device_id_type=MESH).wait_recv()

    def finish(self):
        for copy, is_self in self.sent:
            if is_self is None:
                copy.wait_send()
            else:
                pl.when(jnp.logical_not(is_self))(copy.wait_send)


def flip(block):
    return block.astype(F32).T


def kernel(inc_hbm, cot_hbm, w_hbm, rows_hbm, count_ref, gate_hbm, din_ref, wg,
           w, first, rows_ref, gate_ref, cols, flat, part, own, via, xin, d_all, share, yin, ysum, zin, zsum, fin,
           send_sem, recv_sem, w_sem):
    p = lax.axis_index("pipe")
    x = lax.axis_index("dp")
    f = lax.axis_index("fsdp")
    z, y = lax.div(f, NY), lax.rem(f, NY)

    def dev(px, xx, yy, zz):
        return (px, xx, zz * NY + yy)

    def at_x(o):
        return lax.rem(x + o + NX, NX)

    def at_y(o):
        return lax.rem(y + o + NY, NY)

    def at_z(o):
        return lax.rem(z + o + NZ, NZ)

    def to_x(o):
        return dev(p, at_x(o), y, z)

    def to_y(o):
        return dev(p, x, at_y(o), z)

    def to_z(o):
        return dev(p, x, y, at_z(o))

    def slot_of(plane, m, k):
        return lax.rem(2 * plane + NZ + (1 + m if k else -m), NZ)

    def slot_holds(plane, slot):
        back = lax.rem(2 * plane + NZ - slot, NZ)
        k = (back > 3).astype(jnp.int32)
        m = jnp.where(back > 3, NZ - 1 - back, back)
        return lax.rem(plane + m, NX), k

    home_x = lax.div(z, 2)
    away = lax.rem(x - home_x + NX, NX)
    home_z = jnp.where(lax.rem(z, 2) == 1, lax.rem(z + away, NZ), lax.rem(z - away + NZ, NZ))
    from_x, from_k = slot_holds(x, z)
    from_z = 2 * x + from_k
    home_self = home_x == x
    end_z = 2 * x + lax.div(z, NZ // 2)
    fin_self = end_z == z

    barrier = pltpu.get_barrier_semaphore()

    def greet(to):
        pl.semaphore_signal(barrier, inc=1, device_id=to, device_id_type=MESH)

    relay = dev(1 - p, home_x, y, home_z)
    home = dev(p, home_x, y, home_z)
    greet(relay)
    greet(dev(1 - p, from_x, y, from_z))

    @pl.when(jnp.logical_not(home_self))
    def _():
        greet(home)
        greet(dev(p, from_x, y, from_z))
    for o in range(1, NX):
        greet(to_x(o))
    for o in range(1, NY):
        greet(to_y(o))
    for o in range(1, NZ):
        greet(to_z(o))
    for j in range(4):
        to = dev(p, at_x(j), y, end_z)
        if j == 0:
            pl.when(jnp.logical_not(fin_self))(functools.partial(greet, to))
        else:
            greet(to)
        src_z = 4 * lax.rem(z, 2) + j
        same = jnp.logical_and(home_x == x, src_z == z)
        pl.when(jnp.logical_not(same))(functools.partial(greet, dev(p, home_x, y, src_z)))

    small = [pltpu.make_async_copy(cot_hbm, first.at[0], w_sem.at[3]),
             pltpu.make_async_copy(rows_hbm, rows_ref, w_sem.at[4]),
             pltpu.make_async_copy(gate_hbm, gate_ref, w_sem.at[5])]
    w_copies = [pltpu.make_async_copy(w_hbm.at[0, i], w.at[i], w_sem.at[i]) for i in range(3)]
    for copy in small + w_copies:
        copy.start()
    expected = 2 + (NX - 1) + (NY - 1) + (NZ - 1) + 8
    pl.semaphore_wait(barrier, expected + jnp.where(home_self, 0, 2) - jnp.where(fin_self, 2, 0))

    links = Links(send_sem, recv_sem, to_z(1))
    put, take = links.put, links.take

    put(("home", 0), inc_hbm, cols.at[0, home_z, y], relay)

    for copy in small:
        copy.wait()

    down = lax.broadcasted_iota(jnp.int32, (TOK, TOK), 0)
    across = lax.broadcasted_iota(jnp.int32, (TOK, TOK), 1)
    named = jnp.sum(jnp.where(down == across, rows_ref[...], 0).astype(F32), axis=1, keepdims=True)
    routed_here = jnp.logical_and(named == across.astype(F32), down < count_ref[...])
    live = jnp.sum(jnp.where(routed_here, 1.0, 0.0), axis=0, keepdims=True) > 0.5
    first[1] = jnp.where(live, gate_ref[...] * first[0].astype(F32), 0.0).astype(BF16)

    low = pl.ds(0, CUT)
    high = pl.ds(CUT, COLS - CUT)

    def gather_steps(a):
        buf = cols.at[a]
        mid = CUT + 16 * ((COLS - CUT + 16) // 32)
        halves = (pl.ds(CUT, mid - CUT), pl.ds(mid, COLS - mid))

        def piece(j, o=0, rows=high):
            return buf.at[at_z(j), at_y(o), rows]

        def send_z(name, j, d, o, rows):
            put((name, a, (j - d) % NZ, o, rows.start), piece(j, o, rows), piece(j, o, rows), to_z(d))

        def take_z(name, j, o, rows):
            take((name, a, j % NZ, o, rows.start), piece(j, o, rows))

        def spread(j):
            for o in (2, 1, 3):
                put(("y", a, NY - o, j % NZ), piece(j), piece(j), to_y(o))

        def hop_out(o, rows):
            for d in (2, -2, 1, -1):
                send_z("z", 0, d, o, rows)

        def hop_on(o, rows, j):
            take_z("z", j, o, rows)
            d = 1 if j < 0 else -1
            send_z("z", j, d, o, rows)
            if rows is low:
                if (j < 0) == (o < 2):
                    send_z("z", j, 2 * d, o, rows)
            else:
                send_z("z", j, 2 * d, o, halves[0] if j < 0 else halves[1])

        def start():
            take(("home", a), buf.at[z, y])
            hop_out(0, high)
            for o in (2, 1, 3):
                put(("ly", a, NY - o), piece(0, 0, low), piece(0, 0, low), to_y(o))
            hop_out(0, low)
            spread(0)

        def first_hop():
            hop_on(0, high, -2)
            hop_on(0, high, 2)
            for o in (1, 3, 2):
                take(("ly", a, o), piece(0, o, low))
                hop_out(o, low)
            spread(-2)
            spread(2)
            for j in (-1, 1):
                take_z("z", j, 0, high)
                spread(j)
            hop_on(0, low, -2)
            hop_on(0, low, 2)

        def second_hop():
            for j in (-3, 3):
                take_z("z", j, 0, high)
                spread(j)
            for rows in halves:
                take_z("z", 4, 0, rows)
            spread(4)
            for o in (1, 3, 2):
                hop_on(o, low, -2)
                hop_on(o, low, 2)

        def close():
            for j in (0, -2, 2, -1, 1, -3, 3, 4):
                if j in (-1, 1, -3, 3, 4):
                    for o in (0, 1, 3, 2):
                        take_z("z", j, o, low)
                for o in (1, 3, 2):
                    take(("y", a, o, j % NZ), piece(j, o))
                flatten(a, at_z(j))

        return [start, first_hop, second_hop, close]

    def flatten(a, slot):
        turned = flip(cols[a, slot].reshape(NY * COLS, TOK)).astype(BF16)
        g, k = slot_holds(x, slot)
        flat[k, pl.ds(pl.multiple_of(g * TOK, TOK), TOK), :] = turned

    def project(i):
        for t in range(2):
            span = slice(t * 256, t * 256 + 256)
            out = jnp.dot(flat[0], w[i, 0:768, span], preferred_element_type=F32)
            out = out + jnp.dot(flat[1], w[i, 768:1536, span], preferred_element_type=F32)
            part[:, i, :, span] = out.astype(BF16).reshape(NX, TOK, 256)

    upper, lower = pl.ds(0, TOK // 2), pl.ds(TOK // 2, TOK // 2)

    def part_out(i):
        put(("via", i, 3), part.at[at_x(2), i, upper], via.at[0, i], to_x(1))
        put(("via", i, 1), part.at[at_x(2), i, lower], via.at[1, i], to_x(-1))
        put(("part", i, 3, 1), part.at[at_x(1), i, lower], xin.at[0, i, lower], to_x(1))
        put(("part", i, 1, 0), part.at[at_x(-1), i, upper], xin.at[1, i, upper], to_x(-1))

    def part_on(i):
        take(("via", i, 3), via.at[0, i])
        right = part[at_x(1), i, 0:64].astype(F32) + via[0, i].astype(F32)
        part[at_x(1), i, 0:64] = right.astype(BF16)
        put(("part", i, 3, 0), part.at[at_x(1), i, upper], xin.at[0, i, upper], to_x(1))
        take(("via", i, 1), via.at[1, i])
        left = part[at_x(-1), i, 64:128].astype(F32) + via[1, i].astype(F32)
        part[at_x(-1), i, 64:128] = left.astype(BF16)
        put(("part", i, 1, 1), part.at[at_x(-1), i, lower], xin.at[1, i, lower], to_x(-1))

    def total(i):
        take(("part", i, 3, 1), xin.at[0, i, lower])
        take(("part", i, 1, 0), xin.at[1, i, upper])
        take(("part", i, 3, 0), xin.at[0, i, upper])
        take(("part", i, 1, 1), xin.at[1, i, lower])
        return part[x, i].astype(F32) + xin[0, i].astype(F32) + xin[1, i].astype(F32)

    def rows_of(o, lo, n, rows):
        return d_all.at[at_x(o), pl.ds(lo, n), rows]

    def rows_out(lo, n):
        for first_half in (True, False):
            for o in (1, -1):
                rows = upper if (o == 1) == first_half else lower
                put(("row", lo, NX - 1 if o == 1 else 1, first_half), rows_of(0, lo, n, rows), rows_of(0, lo, n, rows), to_x(o))

    def rows_on(lo, n):
        for o, rows in ((-1, upper), (1, lower)):
            take(("row", lo, o % NX, True), rows_of(o, lo, n, rows))
            put(("far", lo, o), rows_of(o, lo, n, rows), rows_of(o, lo, n, rows), to_x(-o))
        for o, rows in ((-1, lower), (1, upper)):
            take(("row", lo, o % NX, False), rows_of(o, lo, n, rows))

    def rows_far(lo, n):
        for o, rows in ((-1, upper), (1, lower)):
            take(("far", lo, o), rows_of(2, lo, n, rows))

    routed_steps, scaled_steps = gather_steps(0), gather_steps(1)
    routed_steps[0]()
    put(("home", 1), first.at[1], cols.at[1, home_z, y], home, home_self)
    routed_steps[1]()
    scaled_steps[0]()
    routed_steps[2]()
    scaled_steps[1]()
    for copy in w_copies:
        copy.wait()
    routed_steps[3]()
    project(0)
    part_out(0)
    project(1)
    part_out(1)
    scaled_steps[2]()
    part_on(0)
    part_on(1)
    scaled_steps[3]()
    project(2)
    part_out(2)

    g_pre = total(0)
    u_pre = total(1)
    sigma = 1.0 / (1.0 + jnp.exp(-g_pre))
    silu = g_pre * sigma
    d_all[x, 2] = (silu * u_pre).astype(BF16)
    own[0] = u_pre * sigma * (1.0 + g_pre * (1.0 - sigma))
    own[1] = silu
    part_on(2)
    d_act = total(2)
    d_all[x, 0] = (d_act * own[0]).astype(BF16)
    d_all[x, 1] = (d_act * own[1]).astype(BF16)
    rows_out(0, 2)

    nt = (((1,), (1,)), ((), ()))

    def make_share(n, g):
        for k in range(2):
            rows = slice(768 * k, 768 * k + 768)
            out = lax.dot_general(w[0, rows], d_all[g, 0], nt, preferred_element_type=F32)
            out = out + lax.dot_general(w[1, rows], d_all[g, 1], nt, preferred_element_type=F32)
            share[n, k] = out.astype(BF16).reshape(NY, COLS, TOK)
        if n == 3:
            for o in (2, 1, 3):
                put(("sy", n, NY - o), share.at[n, :, at_y(o)], yin.at[n, NY - o - 1], to_y(o))
        else:
            put(("sv", n, 3), share.at[n, 0, at_y(2)], yin.at[n, 1, 0], to_y(1))
            put(("sv", n, 1), share.at[n, 1, at_y(2)], yin.at[n, 1, 1], to_y(-1))
            put(("sy", n, 3, 1), share.at[n, 1, at_y(1)], yin.at[n, 2, 1], to_y(1))
            put(("sy", n, 1, 0), share.at[n, 0, at_y(-1)], yin.at[n, 0, 0], to_y(-1))

    def share_on(n):
        for k, o in ((0, 1), (1, -1)):
            take(("sv", n, 2 + o if k == 0 else 1), yin.at[n, 1, k])
            out = share[n, k, at_y(o)].astype(F32) + yin[n, 1, k].astype(F32)
            share[n, k, at_y(o)] = out.astype(BF16)
            put(("sy", n, 3 if o == 1 else 1, k), share.at[n, k, at_y(o)], yin.at[n, 2 if o == 1 else 0, k], to_y(o))

    def reduce_y(n):
        out = share[n, :, y].astype(F32)
        if n == 3:
            for o in range(1, NY):
                take(("sy", n, o), yin.at[n, o - 1])
                out = out + yin[n, o - 1].astype(F32)
        else:
            for o in (1, 3):
                take(("sy", n, o, 0), yin.at[n, o - 1, 0])
                take(("sy", n, o, 1), yin.at[n, o - 1, 1])
                out = out + yin[n, o - 1].astype(F32)
        ysum[n] = out.astype(BF16).reshape(NZ, CHUNK, TOK)
        for o in (4, 3, 5, 2, 6, 1, 7):
            put(("sz", n, NZ - o), ysum.at[n, at_z(o)], zin.at[n, NZ - o - 1], to_z(o))

    def reduce_z(n, o_x):
        out = ysum[n, z].astype(F32)
        for o in range(1, NZ):
            take(("sz", n, o), zin.at[n, o - 1])
            out = out + zin[n, o - 1].astype(F32)
        zsum[n] = out.astype(BF16)
        put(("end",), zsum.at[n], fin.at[lax.rem(z, 4)], dev(p, at_x(o_x), y, end_z),
            fin_self if o_x == 0 else None)

    def weight_grad(i):
        a = 0 if i < 2 else 1
        right = jnp.concatenate([d_all[at_x(m), i] for m in range(NX)], axis=0)
        for k in range(2):
            for q in range(2):
                left = jnp.concatenate(
                    [cols[a, slot_of(x, m, k), pl.ds(2 * q, 2)].reshape(384, TOK) for m in range(NX)], axis=1)
                out = jnp.dot(left, right, preferred_element_type=F32)
                wg[0, i, 768 * k + 384 * q:768 * k + 384 * q + 384] = out.astype(BF16)

    order = (0, 1, 3, 2)
    make_share(0, x)
    rows_on(0, 2)
    rows_out(2, 1)
    share_on(0)
    make_share(1, at_x(1))
    make_share(2, at_x(-1))
    reduce_y(0)
    share_on(1)
    share_on(2)
    rows_far(0, 2)
    make_share(3, at_x(2))
    rows_on(2, 1)
    reduce_y(1)
    reduce_y(2)
    reduce_z(0, order[0])
    weight_grad(0)
    reduce_y(3)
    reduce_z(1, order[1])
    reduce_z(2, order[2])
    weight_grad(1)
    reduce_z(3, order[3])
    rows_far(2, 1)
    weight_grad(2)
    take(("end",), fin)
    din_ref[...] = fin[...].reshape(COLS, TOK)
    links.finish()
    assert len(links.recv_at) <= N_RECV and links.n_sent <= N_SEND


def in_hbm(array):
    return pltpu.with_memory_space_constraint(array, pltpu.HBM)


def on_device(incoming, cotangent, weights, token_rows, row_count, gate):
    vmem = pl.BlockSpec(memory_space=pltpu.VMEM)
    hbm = pl.BlockSpec(memory_space=pltpu.HBM)
    d_input, weight_grad = pl.pallas_call(
        kernel,
        out_shape=(jax.ShapeDtypeStruct((COLS, TOK), BF16),
                   jax.ShapeDtypeStruct((1, 3, ROWS_D, HID), BF16)),
        in_specs=[hbm, hbm, hbm, hbm, vmem, hbm],
        out_specs=(vmem, vmem),
        scratch_shapes=[
            pltpu.VMEM((3, ROWS_D, HID), BF16),
            pltpu.VMEM((2, COLS, TOK), BF16),
            pltpu.VMEM((1, TOK), jnp.int32),
            pltpu.VMEM((1, TOK), F32),
            pltpu.VMEM((2, NZ, NY, COLS, TOK), BF16),
            pltpu.VMEM((2, NX * TOK, ROWS_D // 2), BF16),
            pltpu.VMEM((NX, 3, TOK, HID), BF16),
            pltpu.VMEM((2, TOK, HID), F32),
            pltpu.VMEM((2, 3, TOK // 2, HID), BF16),
            pltpu.VMEM((2, 3, TOK, HID), BF16),
            pltpu.VMEM((NX, 3, TOK, HID), BF16),
            pltpu.VMEM((NX, 2, NY, COLS, TOK), BF16),
            pltpu.VMEM((NX, NY - 1, 2, COLS, TOK), BF16),
            pltpu.VMEM((NX, NZ, CHUNK, TOK), BF16),
            pltpu.VMEM((NX, NZ - 1, CHUNK, TOK), BF16),
            pltpu.VMEM((NX, CHUNK, TOK), BF16),
            pltpu.VMEM((NX, CHUNK, TOK), BF16),
            pltpu.SemaphoreType.DMA((N_SEND,)),
            pltpu.SemaphoreType.DMA((N_RECV,)),
            pltpu.SemaphoreType.DMA((6,)),
        ],
        compiler_params=pltpu.CompilerParams(
            collective_id=0, has_side_effects=True, vmem_limit_bytes=36 << 20),
        cost_estimate=pl.CostEstimate(flops=6_400_000_000, bytes_accessed=10_000_000, transcendentals=65536),
        name="expert",
    )(in_hbm(incoming.T), in_hbm(cotangent.T), in_hbm(weights), in_hbm(token_rows.reshape(1, TOK)),
      row_count.reshape(1, 1), in_hbm(gate.reshape(1, TOK)))
    return d_input.T, weight_grad


def solution(mesh):
    return jax.shard_map(
        on_device,
        mesh=mesh,
        in_specs=(
            P(("pipe", "dp"), "fsdp"),
            P(("pipe", "dp"), "fsdp"),
            P("pipe", None, "dp", "fsdp"),
            P(("pipe", "dp")),
            P(("pipe", "dp")),
            P(("pipe", "dp")),
        ),
        out_specs=(P(("pipe", "dp"), "fsdp"), P("pipe", None, "dp", "fsdp")),
        check_vma=False,
    )
```
